256 devices in a mesh: ctx: 32 (over x, z), ch: 8 (over y, core).
Axes of the slice: x: 4, y: 4, z: 8, core: 2. Of those that a mesh axis runs over, the one named last changes fastest.
Arguments:
- tokens: bfloat16 [32768, 8192], P('ctx', 'ch'), may hold values from -6 to 6
- in_proj: bfloat16 [3, 8192, 256], P(None, 'ch'), may hold values from -0.09375 to 0.09375
- short_taps: float32 [256, 3, 3], P('ch'), may hold values from -3.5 to 3.5
- long_filter: float32 [256, 32768], P('ch', 'ctx'), may hold values from -4 to 4
- skip_gain: float32 [256], P('ch'), may hold values from 0.5 to 1.5
- out_proj: bfloat16 [256, 8192], P(None, 'ch'), may hold values from -0.375 to 0.375
Outputs:
- operator_out: bfloat16 [32768, 8192], P('ctx', 'ch')
The draws below stay inside these ranges and needn't reach their ends.
All inputs are finite; a program needn't handle non-finite values.
Results may differ from the reference program's by a relative error of at most 0.0049.
Values may be sent and summed in bfloat16 or wider, within the bound.
A program may use at most 64 MiB of HBM per device.

```python
import math
import jax
import jax.numpy as jnp

D = 8192
GROUP = 256
SHORT = 3
SEQ = 32768


def envelope(rate, sample_offsets):
    height = jnp.sqrt(jnp.expm1(-2.0 * rate) / jnp.expm1(-2.0 * rate * SEQ))
    return height * jnp.exp(-rate * sample_offsets)


def draw_long_filter(key, part):
    key = jax.random.fold_in(key, 7)
    noise_key, pick_key, slow_key, fast_key, spot_key, drop_key, tail_key, share_key = jax.random.split(key, 8)
    slow_share = 0.5
    random_wobble = jnp.clip(jax.random.normal(noise_key, (GROUP, SEQ), jnp.float32), -4.0, 4.0)
    picked = jax.random.uniform(pick_key, (GROUP, 1), jnp.float32) < slow_share
    slow_rate = jnp.exp(jax.random.uniform(slow_key, (GROUP, 1), jnp.float32, math.log(0.2 / SEQ), math.log(2.0 / SEQ)))
    fast_rate = jnp.exp(jax.random.uniform(fast_key, (GROUP, 1), jnp.float32, math.log(8.0 / SEQ), math.log(1.0 / 30.0)))
    falloff_speed = jnp.where(picked, slow_rate, fast_rate)
    tail_rate = jnp.exp(jax.random.uniform(tail_key, (GROUP, 1), jnp.float32, math.log(0.2 / SEQ), math.log(2.0 / SEQ)))
    tail_weight = jax.random.uniform(share_key, (GROUP, 1), jnp.float32, 0.2, 0.35)
    sample_offsets = jnp.arange(SEQ, dtype=jnp.float32)[None, :]
    marked_locations = jax.random.randint(spot_key, (GROUP, 2), 0, SEQ).astype(jnp.float32)
    dropped_samples = jax.random.uniform(drop_key, (GROUP, 2), jnp.float32, 0.5, 0.8)
    spike_train = jnp.where(sample_offsets >= marked_locations[:, 0:1], dropped_samples[:, 0:1], 1.0) * jnp.where(sample_offsets >= marked_locations[:, 1:2], dropped_samples[:, 1:2], 1.0)
    mixed_envelope = jnp.sqrt(1.0 - tail_weight) * envelope(falloff_speed, sample_offsets) + jnp.sqrt(tail_weight) * envelope(tail_rate, sample_offsets)
    return random_wobble * mixed_envelope * spike_train


def raised(drawn, rng, source, target, blocks, factor):
    def block_of(axis_at):
        return (jnp.arange(drawn.shape[axis_at]) // (drawn.shape[axis_at] // blocks)).reshape((-1,) + (1,) * (drawn.ndim - 1 - axis_at))

    one_side = jax.random.permutation(rng, blocks)[block_of(target)]
    other_side = (block_of(target) + blocks // 2) % blocks
    return jnp.where((block_of(source) == one_side) | (block_of(source) == other_side), factor * drawn, drawn)


def level_of(own_key, dims, cuts, low, high):
    loudness, own = 1.0, jax.random.fold_in(own_key, 6)
    for axis_at, parts in cuts:
        draws = jnp.exp(jax.random.uniform(jax.random.fold_in(own, axis_at), (parts,), jnp.float32, low / len(cuts), high / len(cuts)))
        loudness = loudness * jnp.repeat(draws, dims[axis_at] // parts).reshape([-1 if axis == axis_at else 1 for axis in range(len(dims))])
    return loudness


def centred(stream_key, extent, spread, limit, cuts=(), held_as=jnp.bfloat16):
    array = jax.random.normal(stream_key, extent, jnp.float32) * spread
    if len(cuts) > 0:
        array = level_of(stream_key, extent, cuts, -0.22, 0.18) * array
    return jnp.clip(array, min=-limit, max=limit).astype(held_as)


def bell_draw_with(key, extent, deviation, limit, cuts, heavy, kind=jnp.bfloat16):
    drawn = deviation * jax.random.normal(key, extent, jnp.float32)
    if cuts:
        drawn = drawn * level_of(key, extent, cuts, -0.22, 0.18)
    return jnp.clip(raised(drawn, jax.random.fold_in(key, 3), *heavy), -limit, limit).astype(kind)


def setup_inputs(seed: int = 0) -> dict:
    key_of = jax.random.split(jax.random.key(seed), 7)
    return {
        "tokens": centred(key_of[0], (SEQ, D), 1.0, 6.0, ((0, 32), (1, 8))),
        "in_proj": bell_draw_with(key_of[1], (3, D, GROUP), D ** -0.5, 0.09375, ((1, 8),), (1, 2, 8, 2.0)),
        "short_taps": centred(key_of[2], (GROUP, 3, SHORT), SHORT ** -0.5, 3.5, ((0, 8),), jnp.float32),
        "long_filter": draw_long_filter(jax.random.fold_in(key_of[6], 71), 0),
        "skip_gain": jnp.clip(0.5 + 1.0 * jax.random.uniform(key_of[4], (GROUP,), jnp.float32) ** level_of(key_of[4], (GROUP,), ((0, 8),), -0.2, 0.2), 0.5, 1.5),
        "out_proj": centred(key_of[5], (GROUP, D), GROUP ** -0.5, 0.375, ((1, 8),)),
    }


def reference(tokens, in_proj, short_taps, long_filter, skip_gain, out_proj):
    flat_proj = jnp.transpose(in_proj, (1, 0, 2)).reshape(D, 3 * GROUP)
    projected = jnp.dot(tokens, flat_proj, preferred_element_type=jnp.float32)
    projected = jnp.transpose(projected.reshape(SEQ, 3, GROUP), (2, 1, 0))
    padded = jnp.pad(projected, ((0, 0), (0, 0), (SHORT - 1, 0)))
    featured = jnp.zeros_like(projected)
    for lag in range(SHORT):
        featured = featured + short_taps[:, :, lag, None] * padded[:, :, SHORT - 1 - lag:SHORT - 1 - lag + SEQ]
    outer_gate = featured[:, 0]
    carried = featured[:, 1] * featured[:, 2]
    spec_signal = jnp.fft.rfft(carried, n=2 * SEQ, axis=1)
    spec_filter = jnp.fft.rfft(long_filter, n=2 * SEQ, axis=1)
    convolved = jnp.fft.irfft(spec_signal * spec_filter, n=2 * SEQ, axis=1)[:, :SEQ]
    convolved = convolved.astype(jnp.float32)
    gated = (outer_gate * (convolved + skip_gain[:, None] * carried)).astype(jnp.bfloat16)
    return jnp.dot(gated.T, out_proj, preferred_element_type=jnp.float32).astype(jnp.bfloat16)
```

```python
import functools

import jax
import jax.numpy as jnp
import ml_dtypes
import numpy as np
from jax import lax
from jax.experimental import pallas as pl
from jax.experimental.pallas import tpu as pltpu
from jax.sharding import PartitionSpec as P

MESH = pl.DeviceIdType.MESH
BF = jnp.bfloat16
F32 = jnp.float32
NCTX = 32
NY = 4
CH = 32
TOK = 1024
HALF = 512
ROWS = 256
LANE = 128


def split_np(table):
    high = table.astype(ml_dtypes.bfloat16)
    low = (table - high.astype(np.float64)).astype(ml_dtypes.bfloat16)
    return high, low


def tables():
    n1 = np.arange(256)
    k1 = np.arange(256) + 0.5
    angle = 2 * np.pi * np.outer(k1, n1) / 512
    first = np.concatenate([np.cos(angle), -np.sin(angle)], axis=0)
    last = first.T
    n2 = np.arange(128)
    angle = 2 * np.pi * np.outer(n2, n2) / 128
    c, s = np.cos(angle), np.sin(angle)
    forward = np.block([[c, -s], [s, c]])
    backward = np.block([[c, s], [-s, c]])
    angle = 2 * np.pi * np.outer(k1, n2) / 65536
    twist = np.stack([np.cos(angle), -np.sin(angle)]).astype(np.float32)
    return (
        np.stack(split_np(first)),
        np.stack(split_np(last)),
        np.stack(split_np(forward) + split_np(backward)),
        twist,
    )


def dot(a, b, dims=((1,), (0,))):
    return lax.dot_general(a, b, (dims, ((), ())), preferred_element_type=F32)


def split(value):
    high = value.astype(BF)
    return high, (value - high.astype(F32)).astype(BF)


def forward_transform(x, first, mid, twist):
    high, low = split(x)
    both = dot(first[0], jnp.concatenate([high, low], axis=1))
    a = both[:, :LANE] + both[:, LANE:] + dot(first[1], high)
    re, im = a[:ROWS], a[ROWS:]
    cos, sin = twist[0], twist[1]
    turned = jnp.concatenate([re * cos - im * sin, re * sin + im * cos], axis=1)
    high, low = split(turned)
    return dot(high, mid[0]) + (dot(low, mid[0]) + dot(high, mid[1]))


def inverse_transform(re, im, last, mid, twist):
    high, low = split(jnp.concatenate([re, im], axis=1))
    z = dot(high, mid[2]) + (dot(low, mid[2]) + dot(high, mid[3]))
    re, im = z[:, :LANE], z[:, LANE:]
    cos, sin = twist[0], twist[1]
    turned = jnp.concatenate([re * cos + im * sin, im * cos - re * sin], axis=0)
    high, low = split(turned)
    both = dot(last[0], jnp.concatenate([high, low], axis=1))
    return both[:, :LANE] + both[:, LANE:] + dot(last[1], high)


def rows_of(index):
    return pl.ds(pl.multiple_of(index * 8, 8), 8)


def kernel(
    tok_hbm, w_hbm, taps, filt_hbm, skip, first_hbm, last_hbm, mid_hbm, twist_hbm, out_ref,
    tok, w, wt, filt, first, last, mid, twist,
    part, from_core, y_send, y_recv, part0, from_core0, y_send0, y_recv0,
    proj, halo, halo0, cols, carried, car_rows, filt_rows, x_rows, h_rows, spec, y_rows, back_rows, feat0,
    load_sem, core_send, core_recv, ys_sem, yr_sem, halo_send, halo_recv, a2a_send, a2a_recv, g_send, g_recv,
):
    ctx = lax.axis_index("ctx")
    ch = lax.axis_index("ch")
    y = ch // 2
    core = ch % 2

    def at_y(step):
        return {"ctx": ctx, "ch": lax.rem(y + step, NY) * 2 + core}

    partner = {"ctx": ctx, "ch": y * 2 + 1 - core}

    def at_ctx(index):
        return {"ctx": index, "ch": ch}

    def remote(src, dst, send, recv, device):
        return pltpu.make_async_remote_copy(
            src_ref=src, dst_ref=dst, send_sem=send, recv_sem=recv, device_id=device, device_id_type=MESH
        )

    loads = [
        (w_hbm.at[1], w.at[1]),
        (tok_hbm.at[pl.ds(HALF, HALF)], tok.at[pl.ds(HALF, HALF)]),
        (w_hbm.at[2], w.at[2]),
        (tok_hbm.at[pl.ds(0, HALF)], tok.at[pl.ds(0, HALF)]),
        (w_hbm.at[0], w.at[0]),
        (filt_hbm, filt),
        (first_hbm, first),
        (mid_hbm, mid),
        (twist_hbm, twist),
        (last_hbm, last),
    ]
    loads = [pltpu.make_async_copy(src, dst, load_sem.at[n]) for n, (src, dst) in enumerate(loads)]
    for load in loads:
        load.start()

    barrier = pltpu.get_barrier_semaphore()

    def greet(step, carry):
        pl.semaphore_signal(barrier, inc=1, device_id=at_ctx(lax.rem(ctx + step, NCTX)), device_id_type=MESH)
        return carry

    lax.fori_loop(1, NCTX, greet, 0)
    for step in range(1, NY):
        pl.semaphore_signal(barrier, inc=1, device_id=at_y(step), device_id_type=MESH)
    pl.semaphore_signal(barrier, inc=1, device_id=partner, device_id_type=MESH)

    eye = (
        lax.broadcasted_iota(jnp.int32, (256, 256), 0) == lax.broadcasted_iota(jnp.int32, (256, 256), 1)
    ).astype(F32).astype(BF)

    def transpose_weights(j):
        for block in range(4):
            rows = pl.ds(block * 256, 256)
            wt[j, :, rows] = dot(eye, w[j, rows, :], ((1,), (1,))).astype(BF)

    def project(j, q):
        return dot(wt[j], tok[pl.ds(q * HALF, HALF), :], ((1,), (1,)))

    def project_inner(q):
        for j in (1, 2):
            if q == 1:
                loads[0 if j == 1 else 2].wait()
                transpose_weights(j)
                if j == 1:
                    loads[1].wait()
            value = project(j, q)
            for k in range(8):
                part[q, k % 2, k // 2, j - 1] = value[k * CH:(k + 1) * CH]

    def core_copy(q):
        return remote(part.at[q, 1 - core], from_core.at[q], core_send.at[q], core_recv.at[q], partner)

    def y_copy(q, step):
        return remote(y_send.at[q, step - 1], y_recv.at[q, step - 1], ys_sem.at[q, step - 1], yr_sem.at[q, step - 1],
                      at_y(step))

    def y_copy0(step):
        return remote(y_send0.at[step - 1], y_recv0.at[step - 1], ys_sem.at[2, step - 1], yr_sem.at[2, step - 1],
                      at_y(step))

    project_inner(1)
    pl.semaphore_wait(barrier, NCTX + NY - 1)
    core_copy(1).start()
    loads[3].wait()
    project_inner(0)
    core_copy(0).start()

    for q in (1, 0):
        core_copy(q).wait_recv()
        for step in range(1, NY):
            to = lax.rem(y + step, NY)
            y_send[q, step - 1] = (part[q, core, to] + from_core[q, to]).astype(BF)
            y_copy(q, step).start()

    loads[4].wait()
    transpose_weights(0)
    for q in (1, 0):
        value = project(0, q)
        for k in range(8):
            part0[k % 2, k // 2, :, pl.ds(q * HALF, HALF)] = value[k * CH:(k + 1) * CH]
    core_copy0 = remote(part0.at[1 - core], from_core0, core_send.at[2], core_recv.at[2], partner)
    core_copy0.start()

    def exchange(src, dst, slot):
        def send(step, carry):
            peer = lax.rem(ctx + step, NCTX)
            remote(src.at[rows_of(peer)], dst.at[rows_of(ctx)], a2a_send.at[slot], a2a_recv.at[slot],
                   at_ctx(peer)).start()
            return carry

        lax.fori_loop(1, NCTX, send, 0)
        dst[rows_of(ctx), :] = src[rows_of(ctx), :]

    def all_of(src, dst, slot):
        others = pl.ds(0, ROWS - 8)
        return remote(src.at[others], dst.at[others], a2a_send.at[slot], a2a_recv.at[slot],
                      at_ctx(lax.rem(ctx + 1, NCTX)))

    def to_rows(value, dst):
        for g in range(CH // 8):
            for a in range(8):
                dst[pl.ds(64 * g + a, 8, stride=8), :] = value[8 * g:8 * g + 8, LANE * a:LANE * a + LANE]

    loads[5].wait()
    to_rows(filt[...], filt_rows)
    exchange(filt_rows, h_rows, 0)

    core_copy0.wait_recv()
    for step in range(1, NY):
        to = lax.rem(y + step, NY)
        y_send0[step - 1] = part0[core, to] + from_core0[to]
        y_copy0(step).start()

    sublane = lax.broadcasted_iota(jnp.int32, (8, LANE), 0)

    def column(read, slot):
        for g in range(CH // 8):
            value = jnp.full((8, LANE), read(8 * g), F32)
            for r in range(1, 8):
                value = jnp.where(sublane == r, read(8 * g + r), value)
            cols[slot, pl.ds(8 * g, 8), :] = value

    for j in range(3):
        for lag in range(3):
            column(lambda c, j=j, lag=lag: taps[j, lag, c], 3 * j + lag)
    column(lambda c: skip[c], 9)

    def finish_inner(q):
        for step in range(1, NY):
            y_copy(q, step).wait_recv()
        total = part[q, core, y] + from_core[q, y]
        for step in range(1, NY):
            total = total + y_recv[q, step - 1].astype(F32)
        proj[pl.ds(1, 2), :, pl.ds(q * HALF, HALF)] = total

    after = at_ctx(lax.rem(ctx + 1, NCTX))
    finish_inner(1)
    halo_copy = remote(proj.at[pl.ds(1, 2), :, pl.ds(TOK - LANE, LANE)], halo, halo_send.at[0], halo_recv.at[0], after)
    halo_copy.start()

    for n in (6, 7, 8):
        loads[n].wait()
    h_copies = all_of(filt_rows, h_rows, 0)
    h_copies.wait_recv()
    spec[...] = forward_transform(h_rows[...], first, mid, twist) * (2.0 / 65536)

    finish_inner(0)
    halo_copy.wait_recv()
    has_past = (ctx > 0).astype(F32)

    def featured(j, past):
        extended = jnp.concatenate([past * has_past, proj[j]], axis=1)
        total = jnp.zeros((CH, TOK), F32)
        for lag in range(3):
            moved = extended if lag == 0 else pltpu.roll(extended, lag, 1)
            tap = jnp.concatenate([cols[3 * j + lag]] * (TOK // LANE), axis=1)
            total = total + tap * moved[:, LANE:]
        return total

    carried[...] = featured(1, halo[0]) * featured(2, halo[1])
    to_rows(carried[...], car_rows)
    exchange(car_rows, x_rows, 1)

    for step in range(1, NY):
        y_copy0(step).wait_recv()
    total0 = part0[core, y] + from_core0[y]
    for step in range(1, NY):
        total0 = total0 + y_recv0[step - 1]
    proj[0] = total0
    halo_copy0 = remote(proj.at[0, :, pl.ds(TOK - LANE, LANE)], halo0, halo_send.at[1], halo_recv.at[1], after)
    halo_copy0.start()

    loads[9].wait()
    x_copies = all_of(car_rows, x_rows, 1)
    x_copies.wait_recv()
    x_spec = forward_transform(x_rows[...], first, mid, twist)
    xr, xi = x_spec[:, :LANE], x_spec[:, LANE:]
    hr, hi = spec[:, pl.ds(0, LANE)], spec[:, pl.ds(LANE, LANE)]
    y_rows[...] = inverse_transform(xr * hr - xi * hi, xr * hi + xi * hr, last, mid, twist)
    exchange(y_rows, back_rows, 2)

    halo_copy0.wait_recv()
    feat0[...] = featured(0, halo0[...])
    y_copies = all_of(y_rows, back_rows, 2)
    y_copies.wait_recv()
    for g in range(CH // 8):
        for a in range(8):
            rows, lanes = pl.ds(8 * g, 8), pl.ds(LANE * a, LANE)
            conv = back_rows[pl.ds(64 * g + a, 8, stride=8), :]
            feat0[rows, lanes] = feat0[rows, lanes] * (conv + cols[9, rows, :] * carried[rows, lanes])
    out_ref[ch] = feat0[...].astype(BF)

    def gather(slot, send, device):
        return remote(out_ref.at[slot], out_ref.at[slot], g_send.at[send], g_recv.at[send], device)

    sends = [gather(ch, step - 1, at_y(step)) for step in range(1, NY)]
    sends.append(gather(ch, 3, partner))
    for copy in sends:
        copy.start()
    for step in range(1, NY):
        came = lax.rem(y + NY - step, NY) * 2 + core
        gather(came, step - 1, at_y(step)).wait_recv()
        passed = gather(came, 3 + step, partner)
        passed.start()
        sends.append(passed)
    for send in range(3, 7):
        gather(ch, send, partner).wait_recv()

    for copy in sends:
        copy.wait_send()
    for q in range(2):
        core_copy(q).wait_send()
        for step in range(1, NY):
            y_copy(q, step).wait_send()
    core_copy0.wait_send()
    for step in range(1, NY):
        y_copy0(step).wait_send()
    for copy in (halo_copy, halo_copy0, h_copies, x_copies, y_copies):
        copy.wait_send()


def gated_values(tokens, in_proj, short_taps, long_filter, skip_gain):
    first, last, mid, twist = (jnp.asarray(t) for t in tables())
    hbm = pl.BlockSpec(memory_space=pltpu.HBM)
    smem = pl.BlockSpec(memory_space=pltpu.SMEM)
    vmem = pltpu.VMEM
    dma = pltpu.SemaphoreType.DMA
    scratch = [
        vmem((TOK, 1024), BF), vmem((3, 1024, 256), BF), vmem((3, 256, 1024), BF), vmem((CH, TOK), F32),
        vmem(first.shape, BF), vmem(last.shape, BF), vmem(mid.shape, BF), vmem(twist.shape, F32),
        vmem((2, 2, NY, 2, CH, HALF), F32), vmem((2, NY, 2, CH, HALF), F32),
        vmem((2, NY - 1, 2, CH, HALF), BF), vmem((2, NY - 1, 2, CH, HALF), BF),
        vmem((2, NY, CH, TOK), F32), vmem((NY, CH, TOK), F32),
        vmem((NY - 1, CH, TOK), F32), vmem((NY - 1, CH, TOK), F32),
        vmem((3, CH, TOK), F32), vmem((2, CH, LANE), F32), vmem((CH, LANE), F32), vmem((10, CH, LANE), F32),
        vmem((CH, TOK), F32), vmem((ROWS, LANE), F32), vmem((ROWS, LANE), F32), vmem((ROWS, LANE), F32),
        vmem((ROWS, LANE), F32), vmem((ROWS, 2 * LANE), F32), vmem((ROWS, LANE), F32), vmem((ROWS, LANE), F32),
        vmem((CH, TOK), F32),
        dma((10,)), dma((3,)), dma((3,)), dma((3, 3)), dma((3, 3)), dma((2,)), dma((2,)), dma((3,)), dma((3,)),
        dma((7,)), dma((7,)),
    ]
    return pl.pallas_call(
        kernel,
        out_shape=jax.ShapeDtypeStruct((8, CH, TOK), BF),
        in_specs=[hbm, hbm, smem, hbm, smem, hbm, hbm, hbm, hbm],
        out_specs=pl.BlockSpec(memory_space=pltpu.VMEM),
        scratch_shapes=scratch,
        compiler_params=pltpu.CompilerParams(
            collective_id=0, has_side_effects=True, vmem_limit_bytes=63 << 20
        ),
        name="hyena",
    )(tokens, in_proj, jnp.transpose(short_taps, (1, 2, 0)), long_filter, skip_gain, first, last, mid, twist)


def per_device(tokens, in_proj, short_taps, long_filter, skip_gain, out_proj):
    gated = gated_values(tokens, in_proj, short_taps, long_filter, skip_gain).reshape(8 * CH, TOK)
    return jnp.einsum("ct,cd->td", gated, out_proj, preferred_element_type=F32).astype(BF)


def solution(mesh):
    placed = (
        P("ctx", "ch"),
        P(None, "ch", None),
        P("ch", None, None),
        P("ch", "ctx"),
        P("ch"),
        P(None, "ch"),
    )
    return jax.shard_map(
        per_device, mesh=mesh, in_specs=placed, out_specs=P("ctx", "ch"), check_vma=False
    )
```

```python
import functools

import jax
import jax.numpy as jnp
import ml_dtypes
import numpy as np
from jax import lax
from jax.experimental import pallas as pl
from jax.experimental.pallas import tpu as pltpu
from jax.sharding import PartitionSpec as P

MESH = pl.DeviceIdType.MESH
BF = jnp.bfloat16
F32 = jnp.float32
NCTX = 32
NX, NY, NZ = 4, 4, 8
CH = 32
TOK = 1024
PARTS = 4
PART = TOK // PARTS
HALF = TOK // 2
PIECES = 1
PIECE = TOK // PIECES
ROWS = 256
LANE = 128


def split_np(table):
    high = table.astype(ml_dtypes.bfloat16)
    low = (table - high.astype(np.float64)).astype(ml_dtypes.bfloat16)
    return high, low


def tables():
    n1 = np.arange(256)
    k1 = np.arange(256) + 0.5
    angle = 2 * np.pi * np.outer(k1, n1) / 512
    first = np.concatenate([np.cos(angle), -np.sin(angle)], axis=0)
    last = first.T
    n2 = np.arange(128)
    angle = 2 * np.pi * np.outer(n2, n2) / 128
    c, s = np.cos(angle), np.sin(angle)
    forward = np.block([[c, -s], [s, c]])
    backward = np.block([[c, s], [-s, c]])
    angle = 2 * np.pi * np.outer(k1, n2) / 65536
    twist = np.stack([np.cos(angle), -np.sin(angle)]).astype(np.float32)
    return (
        np.stack(split_np(first)),
        np.stack(split_np(last)),
        np.stack(split_np(forward) + split_np(backward)),
        twist,
    )


def dot(a, b, dims=((1,), (0,))):
    return lax.dot_general(a, b, (dims, ((), ())), preferred_element_type=F32)


def split(value):
    high = value.astype(BF)
    return high, (value - high.astype(F32)).astype(BF)


def forward_transform(x, first, mid, twist):
    high, low = split(x)
    both = dot(first[0], jnp.concatenate([high, low], axis=1))
    a = both[:, :LANE] + both[:, LANE:] + dot(first[1], high)
    re, im = a[:ROWS], a[ROWS:]
    cos, sin = twist[0], twist[1]
    turned = jnp.concatenate([re * cos - im * sin, re * sin + im * cos], axis=1)
    high, low = split(turned)
    return dot(high, mid[0]) + (dot(low, mid[0]) + dot(high, mid[1]))


def inverse_transform(re, im, last, mid, twist):
    high, low = split(jnp.concatenate([re, im], axis=1))
    z = dot(high, mid[2]) + (dot(low, mid[2]) + dot(high, mid[3]))
    re, im = z[:, :LANE], z[:, LANE:]
    cos, sin = twist[0], twist[1]
    turned = jnp.concatenate([re * cos + im * sin, im * cos - re * sin], axis=0)
    high, low = split(turned)
    both = dot(last[0], jnp.concatenate([high, low], axis=1))
    return both[:, :LANE] + both[:, LANE:] + dot(last[1], high)


def rows_of(index):
    return pl.ds(pl.multiple_of(index * 8, 8), 8)


def kernel(
    tok_hbm, w_hbm, taps, filt_hbm, skip, first_hbm, last_hbm, mid_hbm, twist_hbm, out_ref,
    tok, w, wt, filt, first, last, mid, twist,
    part, from_core, y_send, y_recv, part0, from_core0, y_send0, y_recv0,
    proj, halo, halo0, cols, carried, car_rows, filt_rows, x_rows, h_rows, spec, y_rows, back_rows, feat0,
    load_sem, core_send, core_recv, ys_sem, yr_sem, halo_send, halo_recv, a2a_send, a2a_recv, g_send, g_recv, ring_sem,
):
    ctx = lax.axis_index("ctx")
    ch = lax.axis_index("ch")
    y = ch // 2
    core = ch % 2

    def at_y(step):
        return {"ctx": ctx, "ch": lax.rem(y + step, NY) * 2 + core}

    partner = {"ctx": ctx, "ch": y * 2 + 1 - core}

    def at_ctx(index):
        return {"ctx": index, "ch": ch}

    def remote(src, dst, send, recv, device):
        return pltpu.make_async_remote_copy(
            src_ref=src, dst_ref=dst, send_sem=send, recv_sem=recv, device_id=device, device_id_type=MESH
        )

    order = tuple(reversed(range(PARTS)))
    loads = [(w_hbm.at[1], w.at[1]), (w_hbm.at[2], w.at[2])]
    loads += [(tok_hbm.at[pl.ds(q * PART, PART)], tok.at[pl.ds(q * PART, PART)]) for q in order]
    loads += [
        (filt_hbm, filt),
        (w_hbm.at[0], w.at[0]),
        (first_hbm, first),
        (mid_hbm, mid),
        (twist_hbm, twist),
        (last_hbm, last),
    ]
    loads = [pltpu.make_async_copy(src, dst, load_sem.at[n]) for n, (src, dst) in enumerate(loads)]
    late = 2 + PARTS
    for load in loads[:late + 1]:
        load.start()

    barrier = pltpu.get_barrier_semaphore()
    x_at = [lax.rem(ctx // NZ + d, NX) for d in range(NX)]
    z_at = [lax.rem(ctx % NZ + d, NZ) for d in range(NZ)]

    def signal(sem, device):
        pl.semaphore_signal(sem, inc=1, device_id=device, device_id_type=MESH)

    def along_x(step):
        return at_ctx(x_at[step] * NZ + z_at[0])

    def along_z(step):
        return at_ctx(x_at[0] * NZ + z_at[step])

    near = [at_y(2), at_y(1), at_y(3), along_z(2), along_z(6), along_x(2), along_z(1), along_z(7), along_x(1), along_x(3)]
    after, before = at_ctx(lax.rem(ctx + 1, NCTX)), at_ctx(lax.rem(ctx + NCTX - 1, NCTX))
    near += [partner, after, before]
    for device in near:
        signal(barrier, device)

    def greet_ring():
        signal(ring_sem.at[0], along_z(2))
        signal(ring_sem.at[0], along_z(6))

    def greet_plane():
        pl.semaphore_wait(ring_sem.at[0], 2)
        for step in (2, 1, 3):
            signal(ring_sem.at[1], along_x(step))

    def wait_plane():
        pl.semaphore_wait(ring_sem.at[1], 3)

    eye = (
        lax.broadcasted_iota(jnp.int32, (256, 256), 0) == lax.broadcasted_iota(jnp.int32, (256, 256), 1)
    ).astype(F32).astype(BF)

    def transpose_weights(j):
        for block in range(4):
            rows = pl.ds(block * 256, 256)
            wt[j, :, rows] = dot(eye, w[j, rows, :], ((1,), (1,))).astype(BF)

    def project(j, start, size):
        return dot(wt[j], tok[pl.ds(start, size), :], ((1,), (1,)))

    def project_inner(q):
        for j in (1, 2):
            value = project(j, q * PART, PART)
            for k in range(8):
                part[q, k % 2, k // 2, j - 1] = value[k * CH:(k + 1) * CH]

    def core_copy(q):
        return remote(part.at[q, 1 - core], from_core.at[q], core_send.at[q], core_recv.at[q], partner)

    def y_copy(q, step):
        return remote(y_send.at[q, step - 1], y_recv.at[q, step - 1], ys_sem.at[q, step - 1], yr_sem.at[q, step - 1],
                      at_y(step))

    def y_copy0(step):
        return remote(y_send0.at[step - 1], y_recv0.at[step - 1], ys_sem.at[PARTS, step - 1], yr_sem.at[PARTS, step - 1],
                      at_y(step))

    def hops(place):
        return min(place[0], NX - place[0]) + min(place[1], NZ - place[1])

    far_first = sorted(((dx, dz) for dx in range(NX) for dz in range(NZ) if dx or dz), key=hops, reverse=True)

    def exchange(src, dst, slot):
        for dx, dz in far_first:
            peer = x_at[dx] * NZ + z_at[dz]
            remote(src.at[rows_of(peer)], dst.at[rows_of(ctx)], a2a_send.at[slot], a2a_recv.at[slot],
                   at_ctx(peer)).start()
        dst[rows_of(ctx), :] = src[rows_of(ctx), :]

    def all_of(src, dst, slot):
        others = pl.ds(0, ROWS - 8)
        return remote(src.at[others], dst.at[others], a2a_send.at[slot], a2a_recv.at[slot],
                      at_ctx(lax.rem(ctx + 1, NCTX)))

    def to_rows(value, dst):
        for g in range(CH // 8):
            for a in range(8):
                dst[pl.ds(64 * g + a, 8, stride=8), :] = value[8 * g:8 * g + 8, LANE * a:LANE * a + LANE]

    def send_chip_sums(q):
        core_copy(q).wait_recv()
        for step in (2, 1, 3):
            to = lax.rem(y + step, NY)
            y_send[q, step - 1] = (part[q, core, to] + from_core[q, to]).astype(BF)
            y_copy(q, step).start()

    for n, j in enumerate((1, 2)):
        loads[n].wait()
        transpose_weights(j)
    for n, q in enumerate(order):
        loads[2 + n].wait()
        project_inner(q)
        if n == 0:
            for load in loads[late + 1:]:
                load.start()
            pl.semaphore_wait(barrier, len(near))
            greet_ring()
        core_copy(q).start()
        if n > 0:
            send_chip_sums(order[n - 1])
    send_chip_sums(order[-1])
    greet_plane()

    loads[late + 1].wait()
    transpose_weights(0)
    for q in range(2):
        value = project(0, q * HALF, HALF)
        for k in range(8):
            part0[k % 2, k // 2, :, pl.ds(q * HALF, HALF)] = value[k * CH:(k + 1) * CH]
    core_copy0 = remote(part0.at[1 - core], from_core0, core_send.at[PARTS], core_recv.at[PARTS], partner)
    core_copy0.start()

    loads[late].wait()
    to_rows(filt[...], filt_rows)

    sublane = lax.broadcasted_iota(jnp.int32, (8, LANE), 0)

    def column(read, slot):
        for g in range(CH // 8):
            value = jnp.full((8, LANE), read(8 * g), F32)
            for r in range(1, 8):
                value = jnp.where(sublane == r, read(8 * g + r), value)
            cols[slot, pl.ds(8 * g, 8), :] = value

    for j in range(3):
        for lag in range(3):
            column(lambda c, j=j, lag=lag: taps[j, lag, c], 3 * j + lag)
    column(lambda c: skip[c], 9)

    def finish_inner(q):
        for step in range(1, NY):
            y_copy(q, step).wait_recv()
        total = part[q, core, y] + from_core[q, y]
        for step in range(1, NY):
            total = total + y_recv[q, step - 1].astype(F32)
        proj[pl.ds(1, 2), :, pl.ds(q * PART, PART)] = total

    finish_inner(order[0])
    halo_copy = remote(proj.at[pl.ds(1, 2), :, pl.ds(TOK - LANE, LANE)], halo, halo_send.at[0], halo_recv.at[0], after)
    halo_copy.start()

    wait_plane()
    exchange(filt_rows, h_rows, 0)
    for q in order[1:]:
        finish_inner(q)
    halo_copy.wait_recv()
    has_past = (ctx > 0).astype(F32)

    def featured(j, past):
        extended = jnp.concatenate([past * has_past, proj[j]], axis=1)
        total = jnp.zeros((CH, TOK), F32)
        for lag in range(3):
            moved = extended if lag == 0 else pltpu.roll(extended, lag, 1)
            tap = jnp.concatenate([cols[3 * j + lag]] * (TOK // LANE), axis=1)
            total = total + tap * moved[:, LANE:]
        return total

    carried[...] = featured(1, halo[0]) * featured(2, halo[1])
    to_rows(carried[...], car_rows)
    exchange(car_rows, x_rows, 1)

    core_copy0.wait_recv()
    for step in (2, 1, 3):
        to = lax.rem(y + step, NY)
        y_send0[step - 1] = part0[core, to] + from_core0[to]
        y_copy0(step).start()
    for load in loads[late + 2:]:
        load.wait()
    h_copies = all_of(filt_rows, h_rows, 0)
    h_copies.wait_recv()
    spec[...] = forward_transform(h_rows[...], first, mid, twist) * (2.0 / 65536)

    x_copies = all_of(car_rows, x_rows, 1)
    x_copies.wait_recv()
    x_spec = forward_transform(x_rows[...], first, mid, twist)
    xr, xi = x_spec[:, :LANE], x_spec[:, LANE:]
    hr, hi = spec[:, pl.ds(0, LANE)], spec[:, pl.ds(LANE, LANE)]
    y_rows[...] = inverse_transform(xr * hr - xi * hi, xr * hi + xi * hr, last, mid, twist)
    exchange(y_rows, back_rows, 2)

    for step in range(1, NY):
        y_copy0(step).wait_recv()
    total0 = part0[core, y] + from_core0[y]
    for step in range(1, NY):
        total0 = total0 + y_recv0[step - 1]
    proj[0] = total0
    halo_copy0 = remote(proj.at[0, :, pl.ds(TOK - LANE, LANE)], halo0, halo_send.at[1], halo_recv.at[1], after)
    halo_copy0.start()
    halo_copy0.wait_recv()
    feat0[...] = featured(0, halo0[...])
    y_copies = all_of(y_rows, back_rows, 2)
    y_copies.wait_recv()
    def gather(q, slot, send, device):
        tile = out_ref.at[slot, :, pl.ds(q * PIECE, PIECE)]
        return remote(tile, tile, g_send.at[q, send], g_recv.at[q, send], device)

    sends = []
    for q in range(PIECES):
        for g in range(CH // 8):
            for a in range(q * PIECE // LANE, (q + 1) * PIECE // LANE):
                rows, lanes = pl.ds(8 * g, 8), pl.ds(LANE * a, LANE)
                conv = back_rows[pl.ds(64 * g + a, 8, stride=8), :]
                feat0[rows, lanes] = feat0[rows, lanes] * (conv + cols[9, rows, :] * carried[rows, lanes])
        lanes = pl.ds(q * PIECE, PIECE)
        out_ref[ch, :, lanes] = feat0[:, lanes].astype(BF)
        sends.append(gather(q, ch, 1, at_y(2)))
        sends[-1].start()
    for q in range(PIECES):
        for step, device in ((1, at_y(1)), (3, at_y(3)), (4, partner)):
            sends.append(gather(q, ch, step - 1, device))
            sends[-1].start()
    for q, step in [(q, 2) for q in range(PIECES)] + [(q, step) for q in range(PIECES) for step in (1, 3)]:
        came = lax.rem(y + NY - step, NY) * 2 + core
        gather(q, came, step - 1, at_y(step)).wait_recv()
        sends.append(gather(q, came, 3 + step, partner))
        sends[-1].start()
    for q in range(PIECES):
        for send in range(3, 7):
            gather(q, ch, send, partner).wait_recv()

    for copy in sends:
        copy.wait_send()
    for q in order:
        core_copy(q).wait_send()
        for step in range(1, NY):
            y_copy(q, step).wait_send()
    core_copy0.wait_send()
    for step in range(1, NY):
        y_copy0(step).wait_send()
    for copy in (halo_copy, halo_copy0, h_copies, x_copies, y_copies):
        copy.wait_send()


def gated_values(tokens, in_proj, short_taps, long_filter, skip_gain):
    first, last, mid, twist = (jnp.asarray(t) for t in tables())
    hbm = pl.BlockSpec(memory_space=pltpu.HBM)
    smem = pl.BlockSpec(memory_space=pltpu.SMEM)
    vmem = pltpu.VMEM
    dma = pltpu.SemaphoreType.DMA
    scratch = [
        vmem((TOK, 1024), BF), vmem((3, 1024, 256), BF), vmem((3, 256, 1024), BF), vmem((CH, TOK), F32),
        vmem(first.shape, BF), vmem(last.shape, BF), vmem(mid.shape, BF), vmem(twist.shape, F32),
        vmem((PARTS, 2, NY, 2, CH, PART), F32), vmem((PARTS, NY, 2, CH, PART), F32),
        vmem((PARTS, NY - 1, 2, CH, PART), BF), vmem((PARTS, NY - 1, 2, CH, PART), BF),
        vmem((2, NY, CH, TOK), F32), vmem((NY, CH, TOK), F32),
        vmem((NY - 1, CH, TOK), F32), vmem((NY - 1, CH, TOK), F32),
        vmem((3, CH, TOK), F32), vmem((2, CH, LANE), F32), vmem((CH, LANE), F32), vmem((10, CH, LANE), F32),
        vmem((CH, TOK), F32), vmem((ROWS, LANE), F32), vmem((ROWS, LANE), F32), vmem((ROWS, LANE), F32),
        vmem((ROWS, LANE), F32), vmem((ROWS, 2 * LANE), F32), vmem((ROWS, LANE), F32), vmem((ROWS, LANE), F32),
        vmem((CH, TOK), F32),
        dma((8 + PARTS,)), dma((PARTS + 1,)), dma((PARTS + 1,)), dma((PARTS + 1, 3)), dma((PARTS + 1, 3)), dma((2,)), dma((2,)), dma((3,)), dma((3,)),
        dma((PIECES, 7)), dma((PIECES, 7)), pltpu.SemaphoreType.REGULAR((2,)),
    ]
    return pl.pallas_call(
        kernel,
        out_shape=pltpu.VMEM((8, CH, TOK), BF),
        in_specs=[hbm, hbm, smem, hbm, smem, hbm, hbm, hbm, hbm],
        out_specs=pl.BlockSpec(memory_space=pltpu.VMEM),
        scratch_shapes=scratch,
        compiler_params=pltpu.CompilerParams(
            collective_id=0, has_side_effects=True, vmem_limit_bytes=62 << 20
        ),
        name="hyena",
    )(tokens, in_proj, jnp.transpose(short_taps, (1, 2, 0)), long_filter, skip_gain, first, last, mid, twist)


def per_device(tokens, in_proj, short_taps, long_filter, skip_gain, out_proj):
    gated = gated_values(tokens, in_proj, short_taps, long_filter, skip_gain).reshape(8 * CH, TOK)
    return jnp.einsum("ct,cd->td", gated, out_proj, preferred_element_type=F32).astype(BF)


def solution(mesh):
    placed = (
        P("ctx", "ch"),
        P(None, "ch", None),
        P("ch", None, None),
        P("ch", "ctx"),
        P("ch"),
        P(None, "ch"),
    )
    return jax.shard_map(
        per_device, mesh=mesh, in_specs=placed, out_specs=P("ctx", "ch"), check_vma=False
    )
```

```python
import functools

import jax
import jax.numpy as jnp
import ml_dtypes
import numpy as np
from jax import lax
from jax.experimental import pallas as pl
from jax.experimental.pallas import tpu as pltpu
from jax.sharding import PartitionSpec as P

MESH = pl.DeviceIdType.MESH
BF = jnp.bfloat16
F32 = jnp.float32
NCTX = 32
NX, NY, NZ = 4, 4, 8
CH = 32
TOK = 1024
PARTS = 4
PART = TOK // PARTS
HALF = TOK // 2
ROWS = 256
LANE = 128


def split_np(table):
    high = table.astype(ml_dtypes.bfloat16)
    low = (table - high.astype(np.float64)).astype(ml_dtypes.bfloat16)
    return high, low


def tables():
    n1 = np.arange(256)
    k1 = np.arange(256) + 0.5
    angle = 2 * np.pi * np.outer(k1, n1) / 512
    first = np.concatenate([np.cos(angle), -np.sin(angle)], axis=0)
    last = first.T
    n2 = np.arange(128)
    angle = 2 * np.pi * np.outer(n2, n2) / 128
    c, s = np.cos(angle), np.sin(angle)
    forward = np.block([[c, -s], [s, c]])
    backward = np.block([[c, s], [-s, c]])
    angle = 2 * np.pi * np.outer(k1, n2) / 65536
    twist = np.stack([np.cos(angle), -np.sin(angle)]).astype(np.float32)
    return (
        np.stack(split_np(first)),
        np.stack(split_np(last)),
        np.stack(split_np(forward) + split_np(backward)),
        twist,
    )


def dot(a, b, dims=((1,), (0,))):
    return lax.dot_general(a, b, (dims, ((), ())), preferred_element_type=F32)


def split(value):
    high = value.astype(BF)
    return high, (value - high.astype(F32)).astype(BF)


def forward_transform(x, first, mid, twist):
    high, low = split(x)
    both = dot(first[0], jnp.concatenate([high, low], axis=1))
    a = both[:, :LANE] + both[:, LANE:] + dot(first[1], high)
    re, im = a[:ROWS], a[ROWS:]
    cos, sin = twist[0], twist[1]
    turned = jnp.concatenate([re * cos - im * sin, re * sin + im * cos], axis=1)
    high, low = split(turned)
    return dot(high, mid[0]) + (dot(low, mid[0]) + dot(high, mid[1]))


def inverse_transform(re, im, last, mid, twist):
    high, low = split(jnp.concatenate([re, im], axis=1))
    z = dot(high, mid[2]) + (dot(low, mid[2]) + dot(high, mid[3]))
    re, im = z[:, :LANE], z[:, LANE:]
    cos, sin = twist[0], twist[1]
    turned = jnp.concatenate([re * cos + im * sin, im * cos - re * sin], axis=0)
    high, low = split(turned)
    both = dot(last[0], jnp.concatenate([high, low], axis=1))
    return both[:, :LANE] + both[:, LANE:] + dot(last[1], high)


def rows_of(index):
    return pl.ds(pl.multiple_of(index * 8, 8), 8)


def kernel(
    tok_hbm, w_hbm, taps, filt_hbm, skip, first_hbm, last_hbm, mid_hbm, twist_hbm, out_ref,
    tok, w, wt, filt, first, last, mid, twist,
    part, from_core, y_send, y_recv, part0, from_core0, y_send0, y_recv0,
    proj, halo, halo0, cols, carried, car_rows, filt_rows, x_rows, h_rows, spec, y_rows, back_rows, feat0,
    load_sem, core_send, core_recv, ys_sem, yr_sem, halo_send, halo_recv, a2a_send, a2a_recv, g_send, g_recv, ring_sem,
):
    ctx = lax.axis_index("ctx")
    ch = lax.axis_index("ch")
    y = ch // 2
    core = ch % 2

    def at_y(step):
        return {"ctx": ctx, "ch": lax.rem(y + step, NY) * 2 + core}

    def other_at_y(step):
        return {"ctx": ctx, "ch": lax.rem(y + step, NY) * 2 + 1 - core}

    partner = {"ctx": ctx, "ch": y * 2 + 1 - core}

    def at_ctx(index):
        return {"ctx": index, "ch": ch}

    def remote(src, dst, send, recv, device):
        return pltpu.make_async_remote_copy(
            src_ref=src, dst_ref=dst, send_sem=send, recv_sem=recv, device_id=device, device_id_type=MESH
        )

    order = tuple(reversed(range(PARTS)))
    loads = [(w_hbm.at[1], w.at[1]), (w_hbm.at[2], w.at[2])]
    loads += [(tok_hbm.at[pl.ds(q * PART, PART)], tok.at[pl.ds(q * PART, PART)]) for q in order]
    loads += [
        (filt_hbm, filt),
        (w_hbm.at[0], w.at[0]),
        (first_hbm, first),
        (mid_hbm, mid),
        (twist_hbm, twist),
        (last_hbm, last),
    ]
    loads = [pltpu.make_async_copy(src, dst, load_sem.at[n]) for n, (src, dst) in enumerate(loads)]
    late = 2 + PARTS
    for load in loads[:late + 1]:
        load.start()

    barrier = pltpu.get_barrier_semaphore()
    x_at = [lax.rem(ctx // NZ + d, NX) for d in range(NX)]
    z_at = [lax.rem(ctx % NZ + d, NZ) for d in range(NZ)]

    def signal(sem, device):
        pl.semaphore_signal(sem, inc=1, device_id=device, device_id_type=MESH)

    def along_x(step):
        return at_ctx(x_at[step] * NZ + z_at[0])

    def along_z(step):
        return at_ctx(x_at[0] * NZ + z_at[step])

    near = [at_y(2), at_y(1), at_y(3), along_z(2), along_z(6), along_x(2), along_z(1), along_z(7), along_x(1), along_x(3)]
    after, before = at_ctx(lax.rem(ctx + 1, NCTX)), at_ctx(lax.rem(ctx + NCTX - 1, NCTX))
    near += [partner, after, before, other_at_y(1), other_at_y(3)]
    for device in near:
        signal(barrier, device)

    def greet_ring():
        signal(ring_sem.at[0], along_z(2))
        signal(ring_sem.at[0], along_z(6))

    def greet_plane():
        pl.semaphore_wait(ring_sem.at[0], 2)
        for step in (2, 1, 3):
            signal(ring_sem.at[1], along_x(step))

    def wait_plane():
        pl.semaphore_wait(ring_sem.at[1], 3)

    eye = (
        lax.broadcasted_iota(jnp.int32, (256, 256), 0) == lax.broadcasted_iota(jnp.int32, (256, 256), 1)
    ).astype(F32).astype(BF)

    def transpose_weights(j):
        for block in range(4):
            rows = pl.ds(block * 256, 256)
            wt[j, :, rows] = dot(eye, w[j, rows, :], ((1,), (1,))).astype(BF)

    def project(j, start, size):
        return dot(wt[j], tok[pl.ds(start, size), :], ((1,), (1,)))

    def project_inner(q):
        for j in (1, 2):
            value = project(j, q * PART, PART)
            for k in range(8):
                part[q, k % 2, k // 2, j - 1] = value[k * CH:(k + 1) * CH]

    def core_copy(q):
        return remote(part.at[q, 1 - core], from_core.at[q], core_send.at[q], core_recv.at[q], partner)

    def y_copy(q, step):
        return remote(y_send.at[q, step - 1], y_recv.at[q, step - 1], ys_sem.at[q, step - 1], yr_sem.at[q, step - 1],
                      at_y(step))

    def y_copy0(step):
        return remote(y_send0.at[step - 1], y_recv0.at[step - 1], ys_sem.at[PARTS, step - 1], yr_sem.at[PARTS, step - 1],
                      at_y(step))

    def hops(place):
        return min(place[0], NX - place[0]) + min(place[1], NZ - place[1])

    far_first = sorted(((dx, dz) for dx in range(NX) for dz in range(NZ) if dx or dz), key=hops, reverse=True)

    def exchange(src, dst, slot):
        for dx, dz in far_first:
            peer = x_at[dx] * NZ + z_at[dz]
            remote(src.at[rows_of(peer)], dst.at[rows_of(ctx)], a2a_send.at[slot], a2a_recv.at[slot],
                   at_ctx(peer)).start()
        dst[rows_of(ctx), :] = src[rows_of(ctx), :]

    def all_of(src, dst, slot):
        others = pl.ds(0, ROWS - 8)
        return remote(src.at[others], dst.at[others], a2a_send.at[slot], a2a_recv.at[slot],
                      at_ctx(lax.rem(ctx + 1, NCTX)))

    def to_rows(value, dst, blocks):
        for g in range(CH // 8):
            for n, a in enumerate(blocks):
                dst[pl.ds(64 * g + a, 8, stride=8), :] = value[8 * g:8 * g + 8, LANE * n:LANE * n + LANE]

    def send_chip_sums(q):
        core_copy(q).wait_recv()
        for step in (2, 1, 3):
            to = lax.rem(y + step, NY)
            y_send[q, step - 1] = (part[q, core, to] + from_core[q, to]).astype(BF)
            y_copy(q, step).start()

    for n, j in enumerate((1, 2)):
        loads[n].wait()
        transpose_weights(j)
    for n, q in enumerate(order):
        loads[2 + n].wait()
        project_inner(q)
        if n == 0:
            for load in loads[late + 1:]:
                load.start()
            pl.semaphore_wait(barrier, len(near))
            greet_ring()
        core_copy(q).start()
        if n > 0:
            send_chip_sums(order[n - 1])
    greet_plane()
    send_chip_sums(order[-1])
    loads[late].wait()
    to_rows(filt[...], filt_rows, range(TOK // LANE))

    sublane = lax.broadcasted_iota(jnp.int32, (8, LANE), 0)

    def column(read, slot):
        for g in range(CH // 8):
            value = jnp.full((8, LANE), read(8 * g), F32)
            for r in range(1, 8):
                value = jnp.where(sublane == r, read(8 * g + r), value)
            cols[slot, pl.ds(8 * g, 8), :] = value

    for j in range(3):
        for lag in range(3):
            column(lambda c, j=j, lag=lag: taps[j, lag, c], 3 * j + lag)
    column(lambda c: skip[c], 9)

    def finish_inner(q):
        for step in range(1, NY):
            y_copy(q, step).wait_recv()
        total = part[q, core, y] + from_core[q, y]
        for step in range(1, NY):
            total = total + y_recv[q, step - 1].astype(F32)
        proj[pl.ds(1, 2), :, pl.ds(q * PART, PART)] = total

    finish_inner(order[0])
    halo_copy = remote(proj.at[pl.ds(1, 2), :, pl.ds(TOK - LANE, LANE)], halo, halo_send.at[0], halo_recv.at[0], after)
    halo_copy.start()

    loads[late + 1].wait()
    transpose_weights(0)
    for q in range(2):
        value = project(0, q * HALF, HALF)
        for k in range(8):
            part0[k % 2, k // 2, :, pl.ds(q * HALF, HALF)] = value[k * CH:(k + 1) * CH]
    core_copy0 = remote(part0.at[1 - core], from_core0, core_send.at[PARTS], core_recv.at[PARTS], partner)
    core_copy0.start()
    wait_plane()
    exchange(filt_rows, h_rows, 0)


    has_past = (ctx > 0).astype(F32)

    def featured(j, q, first_past):
        past = first_past * has_past if q == 0 else proj[j, :, pl.ds(q * PART - LANE, LANE)]
        extended = jnp.concatenate([past, proj[j, :, pl.ds(q * PART, PART)]], axis=1)
        total = jnp.zeros((CH, PART), F32)
        for lag in range(3):
            moved = extended if lag == 0 else pltpu.roll(extended, lag, 1)
            tap = jnp.concatenate([cols[3 * j + lag]] * (PART // LANE), axis=1)
            total = total + tap * moved[:, LANE:]
        return total

    def carry(q):
        value = featured(1, q, halo[0]) * featured(2, q, halo[1])
        carried[:, pl.ds(q * PART, PART)] = value
        to_rows(value, car_rows, range(q * PART // LANE, (q + 1) * PART // LANE))

    for q in order[1:]:
        finish_inner(q)
        carry(q + 1)
    halo_copy.wait_recv()
    carry(0)
    exchange(car_rows, x_rows, 1)

    core_copy0.wait_recv()
    for step in (2, 1, 3):
        to = lax.rem(y + step, NY)
        y_send0[step - 1] = part0[core, to] + from_core0[to]
        y_copy0(step).start()
    for load in loads[late + 2:]:
        load.wait()
    h_copies = all_of(filt_rows, h_rows, 0)
    h_copies.wait_recv()
    spec[...] = forward_transform(h_rows[...], first, mid, twist) * (2.0 / 65536)

    x_copies = all_of(car_rows, x_rows, 1)
    x_copies.wait_recv()
    x_spec = forward_transform(x_rows[...], first, mid, twist)
    xr, xi = x_spec[:, :LANE], x_spec[:, LANE:]
    hr, hi = spec[:, pl.ds(0, LANE)], spec[:, pl.ds(LANE, LANE)]
    y_rows[...] = inverse_transform(xr * hr - xi * hi, xr * hi + xi * hr, last, mid, twist)
    exchange(y_rows, back_rows, 2)

    for step in range(1, NY):
        y_copy0(step).wait_recv()
    total0 = part0[core, y] + from_core0[y]
    for step in range(1, NY):
        total0 = total0 + y_recv0[step - 1]
    proj[0] = total0
    halo_copy0 = remote(proj.at[0, :, pl.ds(TOK - LANE, LANE)], halo0, halo_send.at[1], halo_recv.at[1], after)
    halo_copy0.start()
    halo_copy0.wait_recv()
    for q in range(PARTS):
        feat0[:, pl.ds(q * PART, PART)] = featured(0, q, halo0[...])
    y_copies = all_of(y_rows, back_rows, 2)
    y_copies.wait_recv()
    for g in range(CH // 8):
        for a in range(TOK // LANE):
            rows, lanes = pl.ds(8 * g, 8), pl.ds(LANE * a, LANE)
            conv = back_rows[pl.ds(64 * g + a, 8, stride=8), :]
            feat0[rows, lanes] = feat0[rows, lanes] * (conv + cols[9, rows, :] * carried[rows, lanes])
    out_ref[ch] = feat0[...].astype(BF)

    whole, upper, lower = pl.ds(0, CH), pl.ds(0, CH // 2), pl.ds(CH // 2, CH // 2)

    def gather(slot, rows, lane, device):
        tile = out_ref.at[slot, rows, :]
        return remote(tile, tile, g_send.at[lane], g_recv.at[lane], device)

    sends = [gather(ch, whole, 0, at_y(2)), gather(ch, upper, 1, at_y(1)), gather(ch, upper, 2, at_y(3))]
    sends += [gather(ch, lower, 3, at_y(1)), gather(ch, lower, 4, at_y(3))]
    sends += [gather(ch, lower, 5, other_at_y(1)), gather(ch, lower, 6, other_at_y(3)), gather(ch, whole, 7, partner)]
    for copy in sends:
        copy.start()
    for step, lane, rows in ((1, 1, upper), (3, 2, upper), (2, 0, whole)):
        came = lax.rem(y + NY - step, NY) * 2 + core
        gather(came, rows, lane, partner).wait_recv()
        sends.append(gather(came, rows, 8 + lane, partner))
        sends[-1].start()
    for lane, rows in enumerate((whole, upper, upper, lower, lower, lower, lower, whole, whole, upper, upper)):
        if lane > 2:
            gather(ch, rows, lane, partner).wait_recv()

    for copy in sends:
        copy.wait_send()
    for q in order:
        core_copy(q).wait_send()
        for step in range(1, NY):
            y_copy(q, step).wait_send()
    core_copy0.wait_send()
    for step in range(1, NY):
        y_copy0(step).wait_send()
    for copy in (halo_copy, halo_copy0, h_copies, x_copies, y_copies):
        copy.wait_send()


def gated_values(tokens, in_proj, short_taps, long_filter, skip_gain):
    first, last, mid, twist = (jnp.asarray(t) for t in tables())
    hbm = pl.BlockSpec(memory_space=pltpu.HBM)
    smem = pl.BlockSpec(memory_space=pltpu.SMEM)
    vmem = pltpu.VMEM
    dma = pltpu.SemaphoreType.DMA
    scratch = [
        vmem((TOK, 1024), BF), vmem((3, 1024, 256), BF), vmem((3, 256, 1024), BF), vmem((CH, TOK), F32),
        vmem(first.shape, BF), vmem(last.shape, BF), vmem(mid.shape, BF), vmem(twist.shape, F32),
        vmem((PARTS, 2, NY, 2, CH, PART), F32), vmem((PARTS, NY, 2, CH, PART), F32),
        vmem((PARTS, NY - 1, 2, CH, PART), BF), vmem((PARTS, NY - 1, 2, CH, PART), BF),
        vmem((2, NY, CH, TOK), F32), vmem((NY, CH, TOK), F32),
        vmem((NY - 1, CH, TOK), F32), vmem((NY - 1, CH, TOK), F32),
        vmem((3, CH, TOK), F32), vmem((2, CH, LANE), F32), vmem((CH, LANE), F32), vmem((10, CH, LANE), F32),
        vmem((CH, TOK), F32), vmem((ROWS, LANE), F32), vmem((ROWS, LANE), F32), vmem((ROWS, LANE), F32),
        vmem((ROWS, LANE), F32), vmem((ROWS, 2 * LANE), F32), vmem((ROWS, LANE), F32), vmem((ROWS, LANE), F32),
        vmem((CH, TOK), F32),
        dma((8 + PARTS,)), dma((PARTS + 1,)), dma((PARTS + 1,)), dma((PARTS + 1, 3)), dma((PARTS + 1, 3)), dma((2,)), dma((2,)), dma((3,)), dma((3,)),
        dma((11,)), dma((11,)), pltpu.SemaphoreType.REGULAR((2,)),
    ]
    return pl.pallas_call(
        kernel,
        out_shape=pltpu.VMEM((8, CH, TOK), BF),
        in_specs=[hbm, hbm, smem, hbm, smem, hbm, hbm, hbm, hbm],
        out_specs=pl.BlockSpec(memory_space=pltpu.VMEM),
        scratch_shapes=scratch,
        compiler_params=pltpu.CompilerParams(
            collective_id=0, has_side_effects=True, vmem_limit_bytes=62 << 20
        ),
        name="hyena",
    )(tokens, in_proj, jnp.transpose(short_taps, (1, 2, 0)), long_filter, skip_gain, first, last, mid, twist)


OUT_BLOCKS = 4


def project_out(gated, weights, out_hbm, held, sems):
    size = TOK // OUT_BLOCKS
    copies = []
    for n in range(OUT_BLOCKS):
        rows = pl.ds(n * size, size)
        held[rows, :] = dot(gated[:, rows], weights[...], ((0,), (0,))).astype(BF)
        copies.append(pltpu.make_async_copy(held.at[rows, :], out_hbm.at[rows, :], sems.at[n]))
        copies[-1].start()
    for copy in copies:
        copy.wait()


def per_device(tokens, in_proj, short_taps, long_filter, skip_gain, out_proj):
    gated = gated_values(tokens, in_proj, short_taps, long_filter, skip_gain).reshape(8 * CH, TOK)
    vmem = pl.BlockSpec(memory_space=pltpu.VMEM)
    return pl.pallas_call(
        project_out,
        out_shape=jax.ShapeDtypeStruct((TOK, out_proj.shape[1]), BF),
        in_specs=[vmem, vmem],
        out_specs=pl.BlockSpec(memory_space=pltpu.HBM),
        scratch_shapes=[pltpu.VMEM((TOK, out_proj.shape[1]), BF), pltpu.SemaphoreType.DMA((OUT_BLOCKS,))],
        compiler_params=pltpu.CompilerParams(vmem_limit_bytes=32 << 20),
        name="project_out",
    )(gated, out_proj)


def solution(mesh):
    placed = (
        P("ctx", "ch"),
        P(None, "ch", None),
        P("ch", None, None),
        P("ch", "ctx"),
        P("ch"),
        P(None, "ch"),
    )
    return jax.shard_map(
        per_device, mesh=mesh, in_specs=placed, out_specs=P("ctx", "ch"), check_vma=False
    )
```

```python
import functools

import jax
import jax.numpy as jnp
import ml_dtypes
import numpy as np
from jax import lax
from jax.experimental import pallas as pl
from jax.experimental.pallas import tpu as pltpu
from jax.sharding import PartitionSpec as P

MESH = pl.DeviceIdType.MESH
BF = jnp.bfloat16
F32 = jnp.float32
NCTX = 32
NX, NY, NZ = 4, 4, 8
CH = 32
TOK = 1024
PARTS = 4
PART = TOK // PARTS
HALF = TOK // 2
ROWS = 256
LANE = 128


def split_np(table):
    high = table.astype(ml_dtypes.bfloat16)
    low = (table - high.astype(np.float64)).astype(ml_dtypes.bfloat16)
    return high, low


def tables():
    n1 = np.arange(256)
    k1 = np.arange(256) + 0.5
    angle = 2 * np.pi * np.outer(k1, n1) / 512
    first = np.concatenate([np.cos(angle), -np.sin(angle)], axis=0)
    last = first.T
    n2 = np.arange(128)
    angle = 2 * np.pi * np.outer(n2, n2) / 128
    c, s = np.cos(angle), np.sin(angle)
    forward = np.block([[c, -s], [s, c]])
    backward = np.block([[c, s], [-s, c]])
    angle = 2 * np.pi * np.outer(k1, n2) / 65536
    twist = np.stack([np.cos(angle), -np.sin(angle)]).astype(np.float32)
    return (
        np.stack(split_np(first)),
        np.stack(split_np(last)),
        np.stack(split_np(forward) + split_np(backward)),
        twist,
    )


def dot(a, b, dims=((1,), (0,))):
    return lax.dot_general(a, b, (dims, ((), ())), preferred_element_type=F32)


def split(value):
    high = value.astype(BF)
    return high, (value - high.astype(F32)).astype(BF)


def forward_transform(x, first, mid, twist):
    high, low = split(x)
    both = dot(first[0], jnp.concatenate([high, low], axis=1))
    a = both[:, :LANE] + both[:, LANE:] + dot(first[1], high)
    re, im = a[:ROWS], a[ROWS:]
    cos, sin = twist[0], twist[1]
    turned = jnp.concatenate([re * cos - im * sin, re * sin + im * cos], axis=1)
    high, low = split(turned)
    return dot(high, mid[0]) + (dot(low, mid[0]) + dot(high, mid[1]))


def inverse_transform(re, im, last, mid, twist):
    high, low = split(jnp.concatenate([re, im], axis=1))
    z = dot(high, mid[2]) + (dot(low, mid[2]) + dot(high, mid[3]))
    re, im = z[:, :LANE], z[:, LANE:]
    cos, sin = twist[0], twist[1]
    turned = jnp.concatenate([re * cos + im * sin, im * cos - re * sin], axis=0)
    high, low = split(turned)
    both = dot(last[0], jnp.concatenate([high, low], axis=1))
    return both[:, :LANE] + both[:, LANE:] + dot(last[1], high)


def rows_of(index):
    return pl.ds(pl.multiple_of(index * 8, 8), 8)


def kernel(
    tok_hbm, w_hbm, taps, filt_hbm, skip, first_hbm, last_hbm, mid_hbm, twist_hbm, out_ref,
    tok, w, wt, filt, first, last, mid, twist,
    part, from_core, y_send, y_recv, part0, from_core0, y_send0, y_recv0,
    proj, halo, halo0, cols, carried, car_rows, filt_rows, x_rows, h_rows, spec, y_rows, back_rows, feat0,
    load_sem, core_send, core_recv, ys_sem, yr_sem, halo_send, halo_recv, a2a_send, a2a_recv, g_send, g_recv, ring_sem,
):
    ctx = lax.axis_index("ctx")
    ch = lax.axis_index("ch")
    y = ch // 2
    core = ch % 2

    def at_y(step):
        return {"ctx": ctx, "ch": lax.rem(y + step, NY) * 2 + core}

    def other_at_y(step):
        return {"ctx": ctx, "ch": lax.rem(y + step, NY) * 2 + 1 - core}

    partner = {"ctx": ctx, "ch": y * 2 + 1 - core}

    def at_ctx(index):
        return {"ctx": index, "ch": ch}

    def remote(src, dst, send, recv, device):
        return pltpu.make_async_remote_copy(
            src_ref=src, dst_ref=dst, send_sem=send, recv_sem=recv, device_id=device, device_id_type=MESH
        )

    order = tuple(reversed(range(PARTS)))
    loads = [(w_hbm.at[1], w.at[1]), (w_hbm.at[2], w.at[2])]
    loads += [(tok_hbm.at[pl.ds(q * PART, PART)], tok.at[pl.ds(q * PART, PART)]) for q in order]
    loads += [
        (filt_hbm, filt),
        (w_hbm.at[0], w.at[0]),
        (first_hbm, first),
        (mid_hbm, mid),
        (twist_hbm, twist),
        (last_hbm, last),
    ]
    loads = [pltpu.make_async_copy(src, dst, load_sem.at[n]) for n, (src, dst) in enumerate(loads)]
    late = 2 + PARTS
    for load in loads[:late + 1]:
        load.start()

    barrier = pltpu.get_barrier_semaphore()
    x_at = [lax.rem(ctx // NZ + d, NX) for d in range(NX)]
    z_at = [lax.rem(ctx % NZ + d, NZ) for d in range(NZ)]

    def signal(sem, device):
        pl.semaphore_signal(sem, inc=1, device_id=device, device_id_type=MESH)

    def along_x(step):
        return at_ctx(x_at[step] * NZ + z_at[0])

    def along_z(step):
        return at_ctx(x_at[0] * NZ + z_at[step])

    near = [at_y(2), at_y(1), at_y(3), along_z(2), along_z(6), along_x(2), along_z(1), along_z(7), along_x(1), along_x(3)]
    after, before = at_ctx(lax.rem(ctx + 1, NCTX)), at_ctx(lax.rem(ctx + NCTX - 1, NCTX))
    near += [partner, after, before, other_at_y(1), other_at_y(3)]
    for device in near:
        signal(barrier, device)

    def greet_ring():
        signal(ring_sem.at[0], along_z(2))
        signal(ring_sem.at[0], along_z(6))

    def greet_plane():
        pl.semaphore_wait(ring_sem.at[0], 2)
        for step in (2, 1, 3):
            signal(ring_sem.at[1], along_x(step))

    def wait_plane():
        pl.semaphore_wait(ring_sem.at[1], 3)

    eye = (
        lax.broadcasted_iota(jnp.int32, (256, 256), 0) == lax.broadcasted_iota(jnp.int32, (256, 256), 1)
    ).astype(F32).astype(BF)

    def transpose_weights(j):
        for block in range(4):
            rows = pl.ds(block * 256, 256)
            wt[j, :, rows] = dot(eye, w[j, rows, :], ((1,), (1,))).astype(BF)

    def project(j, start, size):
        return dot(wt[j], tok[pl.ds(start, size), :], ((1,), (1,)))

    def project_inner(q):
        for j in (1, 2):
            value = project(j, q * PART, PART)
            for k in range(8):
                part[q, k % 2, k // 2, j - 1] = value[k * CH:(k + 1) * CH]

    def core_copy(q):
        return remote(part.at[q, 1 - core], from_core.at[q], core_send.at[q], core_recv.at[q], partner)

    def y_copy(q, step):
        return remote(y_send.at[q, step - 1], y_recv.at[q, step - 1], ys_sem.at[q, step - 1], yr_sem.at[q, step - 1],
                      at_y(step))

    def y_copy0(step):
        return remote(y_send0.at[step - 1], y_recv0.at[step - 1], ys_sem.at[PARTS, step - 1], yr_sem.at[PARTS, step - 1],
                      at_y(step))

    def hops(place):
        return min(place[0], NX - place[0]) + min(place[1], NZ - place[1])

    turns = (0, 1, NZ - 1, 2, NZ - 2, 3, NZ - 3, 4)
    far_first = sorted(((dx, dz) for dx in (2, 1, 3, 0) for dz in turns if dx or dz), key=hops, reverse=True)

    def exchange(src, dst, slot):
        for dx, dz in far_first:
            peer = x_at[dx] * NZ + z_at[dz]
            remote(src.at[rows_of(peer)], dst.at[rows_of(ctx)], a2a_send.at[slot], a2a_recv.at[slot],
                   at_ctx(peer)).start()
        dst[rows_of(ctx), :] = src[rows_of(ctx), :]

    def all_of(src, dst, slot):
        others = pl.ds(0, ROWS - 8)
        return remote(src.at[others], dst.at[others], a2a_send.at[slot], a2a_recv.at[slot],
                      at_ctx(lax.rem(ctx + 1, NCTX)))

    def to_rows(value, dst, blocks):
        for g in range(CH // 8):
            for n, a in enumerate(blocks):
                dst[pl.ds(64 * g + a, 8, stride=8), :] = value[8 * g:8 * g + 8, LANE * n:LANE * n + LANE]

    def send_chip_sums(q):
        core_copy(q).wait_recv()
        for step in (2, 1, 3):
            to = lax.rem(y + step, NY)
            y_send[q, step - 1] = (part[q, core, to] + from_core[q, to]).astype(BF)
            y_copy(q, step).start()

    for n, j in enumerate((1, 2)):
        loads[n].wait()
        transpose_weights(j)
    for n, q in enumerate(order):
        loads[2 + n].wait()
        project_inner(q)
        if n == 0:
            for load in loads[late + 1:]:
                load.start()
            pl.semaphore_wait(barrier, len(near))
            greet_ring()
        core_copy(q).start()
        if n > 0:
            send_chip_sums(order[n - 1])
    greet_plane()
    send_chip_sums(order[-1])
    loads[late].wait()
    to_rows(filt[...], filt_rows, range(TOK // LANE))

    sublane = lax.broadcasted_iota(jnp.int32, (8, LANE), 0)

    def column(read, slot):
        for g in range(CH // 8):
            value = jnp.full((8, LANE), read(8 * g), F32)
            for r in range(1, 8):
                value = jnp.where(sublane == r, read(8 * g + r), value)
            cols[slot, pl.ds(8 * g, 8), :] = value

    for j in range(3):
        for lag in range(3):
            column(lambda c, j=j, lag=lag: taps[j, lag, c], 3 * j + lag)
    column(lambda c: skip[c], 9)

    def finish_inner(q):
        for step in range(1, NY):
            y_copy(q, step).wait_recv()
        total = part[q, core, y] + from_core[q, y]
        for step in range(1, NY):
            total = total + y_recv[q, step - 1].astype(F32)
        proj[pl.ds(1, 2), :, pl.ds(q * PART, PART)] = total

    finish_inner(order[0])
    halo_copy = remote(proj.at[pl.ds(1, 2), :, pl.ds(TOK - LANE, LANE)], halo, halo_send.at[0], halo_recv.at[0], after)
    halo_copy.start()

    loads[late + 1].wait()
    transpose_weights(0)
    for q in range(2):
        value = project(0, q * HALF, HALF)
        for k in range(8):
            part0[k % 2, k // 2, :, pl.ds(q * HALF, HALF)] = value[k * CH:(k + 1) * CH]
    core_copy0 = remote(part0.at[1 - core], from_core0, core_send.at[PARTS], core_recv.at[PARTS], partner)
    core_copy0.start()
    wait_plane()
    exchange(filt_rows, h_rows, 0)


    has_past = (ctx > 0).astype(F32)

    def featured(j, q, first_past):
        past = first_past * has_past if q == 0 else proj[j, :, pl.ds(q * PART - LANE, LANE)]
        extended = jnp.concatenate([past, proj[j, :, pl.ds(q * PART, PART)]], axis=1)
        total = jnp.zeros((CH, PART), F32)
        for lag in range(3):
            moved = extended if lag == 0 else pltpu.roll(extended, lag, 1)
            tap = jnp.concatenate([cols[3 * j + lag]] * (PART // LANE), axis=1)
            total = total + tap * moved[:, LANE:]
        return total

    def carry(q):
        value = featured(1, q, halo[0]) * featured(2, q, halo[1])
        carried[:, pl.ds(q * PART, PART)] = value
        to_rows(value, car_rows, range(q * PART // LANE, (q + 1) * PART // LANE))

    for q in order[1:]:
        finish_inner(q)
        carry(q + 1)
    halo_copy.wait_recv()
    carry(0)
    exchange(car_rows, x_rows, 1)

    core_copy0.wait_recv()
    for step in (2, 1, 3):
        to = lax.rem(y + step, NY)
        y_send0[step - 1] = part0[core, to] + from_core0[to]
        y_copy0(step).start()
    for load in loads[late + 2:]:
        load.wait()
    h_copies = all_of(filt_rows, h_rows, 0)
    h_copies.wait_recv()
    spec[...] = forward_transform(h_rows[...], first, mid, twist) * (2.0 / 65536)

    x_copies = all_of(car_rows, x_rows, 1)
    x_copies.wait_recv()
    x_spec = forward_transform(x_rows[...], first, mid, twist)
    xr, xi = x_spec[:, :LANE], x_spec[:, LANE:]
    hr, hi = spec[:, pl.ds(0, LANE)], spec[:, pl.ds(LANE, LANE)]
    y_rows[...] = inverse_transform(xr * hr - xi * hi, xr * hi + xi * hr, last, mid, twist)
    exchange(y_rows, back_rows, 2)

    for step in range(1, NY):
        y_copy0(step).wait_recv()
    total0 = part0[core, y] + from_core0[y]
    for step in range(1, NY):
        total0 = total0 + y_recv0[step - 1]
    proj[0] = total0
    halo_copy0 = remote(proj.at[0, :, pl.ds(TOK - LANE, LANE)], halo0, halo_send.at[1], halo_recv.at[1], after)
    halo_copy0.start()
    halo_copy0.wait_recv()
    for q in range(PARTS):
        feat0[:, pl.ds(q * PART, PART)] = featured(0, q, halo0[...])
    y_copies = all_of(y_rows, back_rows, 2)
    y_copies.wait_recv()
    for g in range(CH // 8):
        for a in range(TOK // LANE):
            rows, lanes = pl.ds(8 * g, 8), pl.ds(LANE * a, LANE)
            conv = back_rows[pl.ds(64 * g + a, 8, stride=8), :]
            feat0[rows, lanes] = feat0[rows, lanes] * (conv + cols[9, rows, :] * carried[rows, lanes])
    out_ref[ch] = feat0[...].astype(BF)

    whole, upper, lower = pl.ds(0, CH), pl.ds(0, CH // 2), pl.ds(CH // 2, CH // 2)

    def gather(slot, rows, lane, device):
        tile = out_ref.at[slot, rows, :]
        return remote(tile, tile, g_send.at[lane], g_recv.at[lane], device)

    sends = [gather(ch, whole, 0, at_y(2)), gather(ch, upper, 1, at_y(1)), gather(ch, upper, 2, at_y(3))]
    sends += [gather(ch, lower, 3, at_y(1)), gather(ch, lower, 4, at_y(3))]
    sends += [gather(ch, lower, 5, other_at_y(1)), gather(ch, lower, 6, other_at_y(3)), gather(ch, whole, 7, partner)]
    for copy in sends:
        copy.start()
    for step, lane, rows in ((1, 1, upper), (3, 2, upper), (2, 0, whole)):
        came = lax.rem(y + NY - step, NY) * 2 + core
        gather(came, rows, lane, partner).wait_recv()
        sends.append(gather(came, rows, 8 + lane, partner))
        sends[-1].start()
    for lane, rows in enumerate((whole, upper, upper, lower, lower, lower, lower, whole, whole, upper, upper)):
        if lane > 2:
            gather(ch, rows, lane, partner).wait_recv()

    for copy in sends:
        copy.wait_send()
    for q in order:
        core_copy(q).wait_send()
        for step in range(1, NY):
            y_copy(q, step).wait_send()
    core_copy0.wait_send()
    for step in range(1, NY):
        y_copy0(step).wait_send()
    for copy in (halo_copy, halo_copy0, h_copies, x_copies, y_copies):
        copy.wait_send()


def gated_values(tokens, in_proj, short_taps, long_filter, skip_gain):
    first, last, mid, twist = (jnp.asarray(t) for t in tables())
    hbm = pl.BlockSpec(memory_space=pltpu.HBM)
    smem = pl.BlockSpec(memory_space=pltpu.SMEM)
    vmem = pltpu.VMEM
    dma = pltpu.SemaphoreType.DMA
    scratch = [
        vmem((TOK, 1024), BF), vmem((3, 1024, 256), BF), vmem((3, 256, 1024), BF), vmem((CH, TOK), F32),
        vmem(first.shape, BF), vmem(last.shape, BF), vmem(mid.shape, BF), vmem(twist.shape, F32),
        vmem((PARTS, 2, NY, 2, CH, PART), F32), vmem((PARTS, NY, 2, CH, PART), F32),
        vmem((PARTS, NY - 1, 2, CH, PART), BF), vmem((PARTS, NY - 1, 2, CH, PART), BF),
        vmem((2, NY, CH, TOK), F32), vmem((NY, CH, TOK), F32),
        vmem((NY - 1, CH, TOK), F32), vmem((NY - 1, CH, TOK), F32),
        vmem((3, CH, TOK), F32), vmem((2, CH, LANE), F32), vmem((CH, LANE), F32), vmem((10, CH, LANE), F32),
        vmem((CH, TOK), F32), vmem((ROWS, LANE), F32), vmem((ROWS, LANE), F32), vmem((ROWS, LANE), F32),
        vmem((ROWS, LANE), F32), vmem((ROWS, 2 * LANE), F32), vmem((ROWS, LANE), F32), vmem((ROWS, LANE), F32),
        vmem((CH, TOK), F32),
        dma((8 + PARTS,)), dma((PARTS + 1,)), dma((PARTS + 1,)), dma((PARTS + 1, 3)), dma((PARTS + 1, 3)), dma((2,)), dma((2,)), dma((3,)), dma((3,)),
        dma((11,)), dma((11,)), pltpu.SemaphoreType.REGULAR((2,)),
    ]
    return pl.pallas_call(
        kernel,
        out_shape=pltpu.VMEM((8, CH, TOK), BF),
        in_specs=[hbm, hbm, smem, hbm, smem, hbm, hbm, hbm, hbm],
        out_specs=pl.BlockSpec(memory_space=pltpu.VMEM),
        scratch_shapes=scratch,
        compiler_params=pltpu.CompilerParams(
            collective_id=0, has_side_effects=True, vmem_limit_bytes=62 << 20
        ),
        name="hyena",
    )(tokens, in_proj, jnp.transpose(short_taps, (1, 2, 0)), long_filter, skip_gain, first, last, mid, twist)


OUT_BLOCKS = 4


def project_out(gated, weights, out_hbm, held, sems):
    size = TOK // OUT_BLOCKS
    copies = []
    for n in range(OUT_BLOCKS):
        rows = pl.ds(n * size, size)
        held[rows, :] = dot(gated[:, rows], weights[...], ((0,), (0,))).astype(BF)
        copies.append(pltpu.make_async_copy(held.at[rows, :], out_hbm.at[rows, :], sems.at[n]))
        copies[-1].start()
    for copy in copies:
        copy.wait()


def per_device(tokens, in_proj, short_taps, long_filter, skip_gain, out_proj):
    gated = gated_values(tokens, in_proj, short_taps, long_filter, skip_gain).reshape(8 * CH, TOK)
    vmem = pl.BlockSpec(memory_space=pltpu.VMEM)
    return pl.pallas_call(
        project_out,
        out_shape=jax.ShapeDtypeStruct((TOK, out_proj.shape[1]), BF),
        in_specs=[vmem, vmem],
        out_specs=pl.BlockSpec(memory_space=pltpu.HBM),
        scratch_shapes=[pltpu.VMEM((TOK, out_proj.shape[1]), BF), pltpu.SemaphoreType.DMA((OUT_BLOCKS,))],
        compiler_params=pltpu.CompilerParams(vmem_limit_bytes=32 << 20),
        name="project_out",
    )(gated, out_proj)


def solution(mesh):
    placed = (
        P("ctx", "ch"),
        P(None, "ch", None),
        P("ch", None, None),
        P("ch", "ctx"),
        P("ch"),
        P(None, "ch"),
    )
    return jax.shard_map(
        per_device, mesh=mesh, in_specs=placed, out_specs=P("ctx", "ch"), check_vma=False
    )
```
